1024 devices in a mesh: dp: 16 (over x, z_hi, core), tensor: 64 (over y, z_lo).
Axes of the slice: x: 4, y: 4, z: 32 (z_hi: 2, z_lo: 16; z = z_hi * 16 + z_lo), core: 2. Of those that a mesh axis runs over, the one named last changes fastest.
Arguments:
- activations: bfloat16 [2048, 29696], P('dp', 'tensor'), may hold values from -6 to 6
- weight_codes: bfloat16 [29696, 7424], P('tensor'), may hold values from -127 to 127, as said below
- channel_scale: float32 [7424], replicated, may hold values from 0.0013130644 to 0.013130643
- output_grads: bfloat16 [2048, 7424], P('dp', 'tensor'), may hold values from -0.375 to 0.375
Outputs:
- input_grads: float32 [2048, 29696], P('dp', 'tensor')
- weight_grads: float32 [29696, 7424], P('tensor', 'dp')
The draws below stay inside these ranges and needn't reach their ends.
Inputs may be any that keep to these rules, and one draw needn't show every extreme that they name: weight_codes holds whole numbers.
All inputs are finite; a program needn't handle non-finite values.
Results may differ from the reference program's by a relative error of at most 0.0029.
Values may be sent and summed in bfloat16 or wider, within the bound.
No kernel may reach another device: no remote copies, remote signals or barrier semaphores. Data moves between devices by JAX's collectives and lax.ppermute only.
A program may use at most 64 MiB of HBM per device.

```python
import math
import jax
import jax.numpy as jnp

D = 7424
FF = 29696
TOKENS = 2048


def draw_weight_codes(key, part):
    key = jax.random.fold_in(key, 7)
    values = jax.random.randint(key, (FF, D), -127, 128)
    return values.astype(jnp.float32).astype(jnp.bfloat16)


def strengthened(values, key, source, target, blocks, factor):
    owner, partner = [(jnp.arange(values.shape[position]) // (values.shape[position] // blocks)).reshape([-1 if axis == position else 1 for axis in range(values.ndim)]) for position in (source, target)]
    chosen = jax.random.permutation(key, blocks)[partner]
    strong = (owner == chosen) | (owner == (partner + blocks // 2) % blocks)
    return jnp.where(strong, factor * values, values)


def shard_levels(stream_key, extent, split, least, top_value):
    def one(dim, blocks):
        heights = jax.random.uniform(jax.random.fold_in(jax.random.fold_in(stream_key, 6), dim), (blocks,), jnp.float32, least / len(split), top_value / len(split))
        return jnp.repeat(jnp.exp(heights), extent[dim] // blocks).reshape((-1,) + (1,) * (len(extent) - dim - 1))

    loudness = one(*split[0])
    for cut in split[1:]:
        loudness = loudness * one(*cut)
    return loudness


def bell_draw(rng, extent, scale, most, shards=(), held_as=jnp.bfloat16):
    array = jax.random.normal(rng, extent, jnp.float32) * scale
    if len(shards) > 0:
        array = shard_levels(rng, extent, shards, -0.22, 0.18) * array
    return jnp.clip(array, min=-most, max=most).astype(held_as)


def gaussian_with(key, dims, deviation, most, shards, heavy, kind=jnp.bfloat16):
    entries = deviation * jax.random.normal(key, dims, jnp.float32)
    if shards:
        entries = entries * shard_levels(key, dims, shards, -0.22, 0.18)
    return jnp.clip(strengthened(entries, jax.random.fold_in(key, 3), *heavy), -most, most).astype(kind)


def setup_inputs(seed: int = 0) -> dict:
    keys = jax.random.split(jax.random.key(seed), 5)
    return {
        "activations": bell_draw(keys[0], (TOKENS, FF), 1.0, 6.0, ((0, 16), (1, 64))),
        "weight_codes": draw_weight_codes(jax.random.fold_in(keys[4], 71), 0),
        "channel_scale": jnp.clip(jnp.exp(jax.random.uniform(keys[2], (D,), jnp.float32, math.log(0.0013130644), math.log(0.013130643))), 0.0013130644, 0.013130643),
        "output_grads": gaussian_with(keys[3], (TOKENS, D), (1 / TOKENS ** 0.5), 0.375, ((0, 16), (1, 64)), (0, 1, 64, 4.0)),
    }


def reference(activations, weight_codes, channel_scale, output_grads):
    scaled = (output_grads.astype(jnp.float32) * channel_scale).astype(jnp.bfloat16)
    input_grads = jnp.dot(scaled, weight_codes.T, preferred_element_type=jnp.float32)
    weight_grads = jnp.dot(activations.T, output_grads, preferred_element_type=jnp.float32)
    return input_grads, weight_grads
```

```python
import itertools

import jax
import jax.numpy as jnp
import numpy as np
from jax import lax
from jax.sharding import Mesh, PartitionSpec as P

AXES = ("x", "zh", "c", "y", "za", "zb")
SIZES = (4, 2, 2, 4, 4, 4)
DP = ("x", "zh", "c")
TENSOR = ("y", "za", "zb")


def permute(value, axes, target):
    sizes = [SIZES[AXES.index(a)] for a in axes]
    pairs = []
    for place in itertools.product(*map(range, sizes)):
        to = target(*place)
        pairs.append((int(np.ravel_multi_index(place, sizes)), int(np.ravel_multi_index(to, sizes))))
    return lax.ppermute(value, axes, pairs)


def spread(value, axis):
    n = SIZES[AXES.index(axis)]
    copies = jnp.broadcast_to(value[None], (n,) + value.shape)
    return lax.all_to_all(copies, axis, 0, 0, tiled=True)


def per_device(activations, weight_codes, channel_scale, output_grads):
    a = activations.T
    g = output_grads.T
    units, tokens = a.shape
    cols = g.shape[0]

    other = permute(a, ("zh",), lambda h: (1 - h,))
    moved = permute(g, AXES, lambda x, zh, c, y, za, zb: (y, za // 2, za % 2, x, zb, 2 * zh + c))

    me = lax.axis_index(TENSOR)
    scale = lax.dynamic_slice(channel_scale, (me * cols,), (cols,))
    scaled = (g.astype(jnp.float32) * scale[:, None]).astype(jnp.bfloat16)

    both = spread(jnp.stack([scaled, moved]), "za")
    rows = both[:, 0].reshape(4 * cols, tokens)
    part = both[:, 1].reshape(4 * cols, tokens)
    both = spread(jnp.concatenate([rows, part]), "zb")
    rows = both[:, : 4 * cols].reshape(4, 4, cols, tokens).transpose(1, 0, 2, 3).reshape(16 * cols, tokens)
    part = both[:, 4 * cols :].reshape(16 * cols, tokens)
    both = spread(jnp.concatenate([rows, part]), "y")
    rows = both[:, : 16 * cols].reshape(64 * cols, tokens)
    part = both[:, 16 * cols :].reshape(16, 4 * cols, tokens)

    input_grads = lax.dot_general(weight_codes, rows, (((1,), (0,)), ((), ())), preferred_element_type=jnp.float32)

    first = lax.axis_index("zh") == 0
    pair = jnp.where(first, jnp.stack([a, other]), jnp.stack([other, a]))
    acts = spread(spread(pair, "x"), "c").transpose(1, 2, 0, 3, 4).reshape(16, units, tokens)
    weight_grads = lax.dot_general(acts, part, (((0, 2), (0, 2)), ((), ())), preferred_element_type=jnp.float32)
    return input_grads.T, weight_grads


def solution(mesh):
    fine = Mesh(mesh.devices.reshape(SIZES), AXES)
    placed = (P(DP, TENSOR), P(TENSOR, None), P(), P(DP, TENSOR))
    return jax.shard_map(
        per_device,
        mesh=fine,
        in_specs=placed,
        out_specs=(P(DP, TENSOR), P(TENSOR, DP)),
        check_vma=False,
    )
```

```python
import itertools

import jax
import jax.numpy as jnp
import numpy as np
from jax import lax
from jax.sharding import Mesh, PartitionSpec as P

AXES = ("x", "zh", "c", "y", "za", "zb")
SIZES = (4, 2, 2, 4, 4, 4)
DP = ("x", "zh", "c")
TENSOR = ("y", "za", "zb")


def permute(value, axes, target):
    sizes = [SIZES[AXES.index(a)] for a in axes]
    pairs = []
    for place in itertools.product(*map(range, sizes)):
        to = target(*place)
        pairs.append((int(np.ravel_multi_index(place, sizes)), int(np.ravel_multi_index(to, sizes))))
    return lax.ppermute(value, axes, pairs)


def along_z(value, step):
    def target(zh, za, zb):
        z = (zh * 16 + za * 4 + zb + step) % 32
        return (z // 16, z % 16 // 4, z % 4)

    return permute(value, ("zh", "za", "zb"), target)


def along_y(value, step):
    return permute(value, ("y",), lambda y: ((y + step) % 4,))


def spread(value, axis):
    n = SIZES[AXES.index(axis)]
    copies = jnp.broadcast_to(value[None], (n,) + value.shape)
    return lax.all_to_all(copies, axis, 0, 0, tiled=True)


def around(own, ahead, opposite, behind):
    y = lax.axis_index("y")
    ring = jnp.broadcast_to(own[None], (4,) + own.shape)
    for k, block in ((1, ahead), (2, opposite), (3, behind)):
        ring = lax.dynamic_update_slice(ring, block[None], ((y + k) % 4, 0, 0))
    return ring


sync = lax.optimization_barrier


def per_device(activations, weight_codes, channel_scale, output_grads):
    a = activations.T
    g = output_grads.T
    units, tokens = a.shape
    cols = g.shape[0]
    cut = units // 2 // 16 * 16
    half = 8 * cols

    me = lax.axis_index(TENSOR)
    scale = lax.dynamic_slice(channel_scale, (me * cols,), (cols,))
    scaled = (g.astype(jnp.float32) * scale[:, None]).astype(jnp.bfloat16)

    part = permute(g, AXES, lambda x, zh, c, y, za, zb: (y, za // 2, za % 2, x, zb, 2 * zh + c))
    rows = spread(scaled, "za").reshape(4 * cols, tokens)
    low = along_z(a[:cut], -1)
    part, rows, low = sync((part, rows, low))

    rows = spread(rows, "zb")
    part = spread(part, "za").reshape(4 * cols, tokens)
    other = jnp.concatenate([along_z(low, -15), along_z(a[cut:], 16)])
    acts = spread(a, "x")
    rows = rows.reshape(4, 4, cols, tokens).transpose(1, 0, 2, 3).reshape(16 * cols, tokens)
    rows, part, other, acts = sync((rows, part, other, acts))

    rows_b, rows_a = along_y(rows, 1), along_y(rows, -1)
    part = spread(part, "zb").reshape(16 * cols, tokens)
    rows_b, rows_a, part, other = sync((rows_b, rows_a, part, other))

    up = along_y(jnp.concatenate([rows_b[:half], part]), 1)
    down = along_y(jnp.concatenate([rows_a[half:], part]), -1)
    acts_o = spread(other, "x")
    up, down, acts_o = sync((up, down, acts_o))
    rows_o = jnp.concatenate([up[:half], down[:half]])
    part_b, part_a = up[half:], down[half:]

    part_o = jnp.concatenate([along_y(part_b[:half], 1), along_y(part_a[half:], -1)])
    first = lax.axis_index("zh") == 0
    acts = jnp.where(first, jnp.stack([acts, acts_o], 1), jnp.stack([acts_o, acts], 1))
    acts_c = permute(acts, ("c",), lambda c: (1 - c,))
    first = lax.axis_index("c") == 0
    acts = jnp.where(first, jnp.stack([acts, acts_c], 2), jnp.stack([acts_c, acts], 2)).reshape(16, units, tokens)

    rows = around(rows, rows_a, rows_o, rows_b).reshape(64 * cols, tokens)
    input_grads = lax.dot_general(weight_codes, rows, (((1,), (0,)), ((), ())), preferred_element_type=jnp.float32)
    part = around(part, part_a, part_o, part_b).reshape(16, 4 * cols, tokens)
    weight_grads = lax.dot_general(acts, part, (((0, 2), (0, 2)), ((), ())), preferred_element_type=jnp.float32)
    return input_grads.T, weight_grads


def solution(mesh):
    fine = Mesh(mesh.devices.reshape(SIZES), AXES)
    placed = (P(DP, TENSOR), P(TENSOR, None), P(), P(DP, TENSOR))
    return jax.shard_map(
        per_device,
        mesh=fine,
        in_specs=placed,
        out_specs=(P(DP, TENSOR), P(TENSOR, DP)),
        check_vma=False,
    )
```

```python
import itertools

import jax
import jax.numpy as jnp
import numpy as np
from jax import lax
from jax.sharding import Mesh, PartitionSpec as P

AXES = ("x", "zh", "c", "y", "za", "zb")
SIZES = (4, 2, 2, 4, 4, 4)
DP = ("x", "zh", "c")
TENSOR = ("y", "za", "zb")


def permute(value, axes, target):
    sizes = [SIZES[AXES.index(a)] for a in axes]
    pairs = []
    for place in itertools.product(*map(range, sizes)):
        to = target(*place)
        pairs.append((int(np.ravel_multi_index(place, sizes)), int(np.ravel_multi_index(to, sizes))))
    return lax.ppermute(value, axes, pairs)


def along_y(value, step):
    return permute(value, ("y",), lambda y: ((y + step) % 4,))


def spread(value, axis):
    n = SIZES[AXES.index(axis)]
    copies = jnp.broadcast_to(value[None], (n,) + value.shape)
    return lax.all_to_all(copies, axis, 0, 0, tiled=True)


def along_zb(value, step):
    return permute(value, ("zb",), lambda zb: ((zb + step) % 4,))


def ordered(axis, blocks):
    me = lax.axis_index(axis)
    ring = jnp.broadcast_to(blocks[0][None], (4,) + blocks[0].shape)
    for k, block in enumerate(blocks[1:], 1):
        ring = lax.dynamic_update_slice(ring, block[None], ((me + k) % 4, 0, 0))
    return ring


sync = lax.optimization_barrier


def per_device(activations, weight_codes, channel_scale, output_grads):
    a = activations.T
    g = output_grads.T
    units, tokens = a.shape
    cols = g.shape[0]
    half = 8 * cols

    me = lax.axis_index(TENSOR)
    scale = lax.dynamic_slice(channel_scale, (me * cols,), (cols,))
    scaled = (g.astype(jnp.float32) * scale[:, None]).astype(jnp.bfloat16)

    part = permute(g, AXES, lambda x, zh, c, y, za, zb: (y, za // 2, za % 2, x, zb, 2 * zh + c))
    other = permute(a, ("zh",), lambda h: (1 - h,))
    rows = spread(scaled, "za").reshape(4 * cols, tokens)
    part, rows, other = sync((part, rows, other))

    part = spread(part, "za").reshape(4 * cols, tokens)
    rows = ordered("zb", [rows] + [along_zb(rows, -k) for k in (1, 2, 3)])
    rows = rows.reshape(4, 4, cols, tokens).transpose(1, 0, 2, 3).reshape(16 * cols, tokens)
    rows, part = sync((rows, part))

    rows_b, rows_a = along_y(rows, 1), along_y(rows, -1)
    part = spread(part, "zb").reshape(16 * cols, tokens)
    rows_b, rows_a, part, other = sync((rows_b, rows_a, part, other))

    up = along_y(jnp.concatenate([rows_b[:half], part]), 1)
    down = along_y(jnp.concatenate([rows_a[half:], part]), -1)
    first = lax.axis_index("zh") == 0
    acts = spread(jnp.where(first, jnp.stack([a, other]), jnp.stack([other, a])), "x")
    up, down, acts = sync((up, down, acts))
    rows_o = jnp.concatenate([up[:half], down[:half]])
    part_b, part_a = up[half:], down[half:]

    part_o = jnp.concatenate([along_y(part_b[:half], 1), along_y(part_a[half:], -1)])
    acts_c = permute(acts, ("c",), lambda c: (1 - c,))
    first = lax.axis_index("c") == 0
    acts = jnp.where(first, jnp.stack([acts, acts_c], 2), jnp.stack([acts_c, acts], 2)).reshape(16, units, tokens)

    rows = ordered("y", [rows, rows_a, rows_o, rows_b]).reshape(64 * cols, tokens)
    input_grads = lax.dot_general(weight_codes, rows, (((1,), (0,)), ((), ())), preferred_element_type=jnp.float32)
    part = ordered("y", [part, part_a, part_o, part_b]).reshape(16, 4 * cols, tokens)
    weight_grads = lax.dot_general(acts, part, (((0, 2), (0, 2)), ((), ())), preferred_element_type=jnp.float32)
    return input_grads.T, weight_grads


def solution(mesh):
    fine = Mesh(mesh.devices.reshape(SIZES), AXES)
    placed = (P(DP, TENSOR), P(TENSOR, None), P(), P(DP, TENSOR))
    return jax.shard_map(
        per_device,
        mesh=fine,
        in_specs=placed,
        out_specs=(P(DP, TENSOR), P(TENSOR, DP)),
        check_vma=False,
    )
```

```python
import itertools

import jax
import jax.numpy as jnp
import numpy as np
from jax import lax
from jax.sharding import Mesh, PartitionSpec as P

AXES = ("x", "zh", "c", "y", "za", "zb")
SIZES = (4, 2, 2, 4, 4, 4)
DP = ("x", "zh", "c")
TENSOR = ("y", "za", "zb")


def permute(value, axes, target):
    sizes = [SIZES[AXES.index(a)] for a in axes]
    pairs = []
    for place in itertools.product(*map(range, sizes)):
        to = target(*place)
        pairs.append((int(np.ravel_multi_index(place, sizes)), int(np.ravel_multi_index(to, sizes))))
    return lax.ppermute(value, axes, pairs)


def along_y(value, step):
    return permute(value, ("y",), lambda y: ((y + step) % 4,))


def spread(value, axis):
    n = SIZES[AXES.index(axis)]
    copies = jnp.broadcast_to(value[None], (n,) + value.shape)
    return lax.all_to_all(copies, axis, 0, 0, tiled=True)


def along_zb(value, step):
    return permute(value, ("zb",), lambda zb: ((zb + step) % 4,))


def ordered(axis, blocks):
    me = lax.axis_index(axis)
    ring = jnp.broadcast_to(blocks[0][None], (4,) + blocks[0].shape)
    for k, block in enumerate(blocks[1:], 1):
        ring = lax.dynamic_update_slice(ring, block[None], ((me + k) % 4, 0, 0))
    return ring


sync = lax.optimization_barrier


def per_device(activations, weight_codes, channel_scale, output_grads):
    a = activations.T
    g = output_grads.T
    units, tokens = a.shape
    cols = g.shape[0]
    half = 8 * cols

    me = lax.axis_index(TENSOR)
    scale = lax.dynamic_slice(channel_scale, (me * cols,), (cols,))
    scaled = (g.astype(jnp.float32) * scale[:, None]).astype(jnp.bfloat16)

    part = permute(g, AXES, lambda x, zh, c, y, za, zb: (y, za // 2, za % 2, x, zb, 2 * zh + c))
    rows = spread(scaled, "za").reshape(4 * cols, tokens)
    part, rows, a = sync((part, rows, a))

    part = spread(part, "za").reshape(4 * cols, tokens)
    rows = ordered("zb", [rows] + [along_zb(rows, -k) for k in (1, 2, 3)])
    rows = rows.reshape(4, 4, cols, tokens).transpose(1, 0, 2, 3).reshape(16 * cols, tokens)
    rows, part, a = sync((rows, part, a))

    rows_b, rows_a = along_y(rows, 1), along_y(rows, -1)
    part = spread(part, "zb").reshape(2, 2, 4 * cols, tokens)
    part = jnp.where(lax.axis_index("c") == 0, part, part[:, ::-1])
    part = jnp.where(lax.axis_index("zh") == 0, part, part[::-1])
    part = part.transpose(1, 0, 2, 3).reshape(16 * cols, tokens)
    rows_b, rows_a, part, a = sync((rows_b, rows_a, part, a))

    up = along_y(jnp.concatenate([rows_b[:half], part]), 1)
    down = along_y(jnp.concatenate([rows_a[half:], part]), -1)
    other = permute(a, ("zh",), lambda h: (1 - h,))
    up, down, a, other = sync((up, down, a, other))
    rows_o = jnp.concatenate([up[:half], down[:half]])
    part_b, part_a = up[half:], down[half:]

    part_o, part_oc = along_y(part_b[:half], 1), along_y(part_a[half:], -1)
    acts = spread(jnp.stack([a, other]), "x")
    part_o, part_oc, acts = sync((part_o, part_oc, acts))
    rows = ordered("y", [rows, rows_a, rows_o, rows_b]).reshape(64 * cols, tokens)
    input_grads = lax.dot_general(weight_codes, rows, (((1,), (0,)), ((), ())), preferred_element_type=jnp.float32)

    acts_c = permute(acts, ("c",), lambda c: (1 - c,))
    weight_grads = 0.0
    for mine, blocks in (
        (acts, [part[:half], part_a[:half], part_o, part_b[:half]]),
        (acts_c, [part[half:], part_a[half:], part_oc, part_b[half:]]),
    ):
        blocks = ordered("y", blocks).reshape(8, 4 * cols, tokens)
        weight_grads += lax.dot_general(
            mine.reshape(8, units, tokens), blocks, (((0, 2), (0, 2)), ((), ())), preferred_element_type=jnp.float32
        )
    return input_grads.T, weight_grads


def solution(mesh):
    fine = Mesh(mesh.devices.reshape(SIZES), AXES)
    placed = (P(DP, TENSOR), P(TENSOR, None), P(), P(DP, TENSOR))
    return jax.shard_map(
        per_device,
        mesh=fine,
        in_specs=placed,
        out_specs=(P(DP, TENSOR), P(TENSOR, DP)),
        check_vma=False,
    )
```

```python
import itertools

import jax
import jax.numpy as jnp
import numpy as np
from jax import lax
from jax.sharding import Mesh, PartitionSpec as P

AXES = ("x", "zh", "c", "y", "za", "zb")
SIZES = (4, 2, 2, 4, 4, 4)
DP = ("x", "zh", "c")
TENSOR = ("y", "za", "zb")


def permute(value, axes, target):
    sizes = [SIZES[AXES.index(a)] for a in axes]
    pairs = []
    for place in itertools.product(*map(range, sizes)):
        to = target(*place)
        pairs.append((int(np.ravel_multi_index(place, sizes)), int(np.ravel_multi_index(to, sizes))))
    return lax.ppermute(value, axes, pairs)


def along_y(value, step):
    return permute(value, ("y",), lambda y: ((y + step) % 4,))


def spread(value, axis):
    n = SIZES[AXES.index(axis)]
    copies = jnp.broadcast_to(value[None], (n,) + value.shape)
    return lax.all_to_all(copies, axis, 0, 0, tiled=True)


def ordered(axis, blocks):
    me = lax.axis_index(axis)
    ring = jnp.broadcast_to(blocks[0][None], (4,) + blocks[0].shape)
    for k, block in enumerate(blocks[1:], 1):
        ring = lax.dynamic_update_slice(ring, block[None], ((me + k) % 4,) + (0,) * block.ndim)
    return ring


sync = lax.optimization_barrier


def per_device(activations, weight_codes, channel_scale, output_grads):
    a = activations.T
    g = output_grads.T
    tokens = a.shape[1]
    cols = g.shape[0]
    half = 8 * cols

    me = lax.axis_index(TENSOR)
    scale = lax.dynamic_slice(channel_scale, (me * cols,), (cols,))
    scaled = (g.astype(jnp.float32) * scale[:, None]).astype(jnp.bfloat16)

    part = permute(g, AXES, lambda x, zh, c, y, za, zb: (y, za // 2, za % 2, x, 2 * zh + c, zb))
    near = spread(a, "x")
    part, near, scaled, a = sync((part, near, scaled, a))

    both = spread(jnp.concatenate([scaled, part]), "za").reshape(8 * cols, tokens)
    both, near, a = sync((both, near, a))

    both = spread(both, "zb").reshape(4, 4, 2, cols, tokens).transpose(2, 1, 0, 3, 4)
    rows = both[0].reshape(2, half, tokens)
    part = both[1].reshape(2, 2, 4 * cols, tokens)
    part = jnp.where(lax.axis_index("c") == 0, part, part[:, ::-1])
    part = jnp.where(lax.axis_index("zh") == 0, part, part[::-1])
    part = part.reshape(2, half, tokens)
    both = jnp.stack([rows, part], 1)
    both, near, a = sync((both, near, a))

    behind, ahead = along_y(both, 1), along_y(both, -1)
    far = permute(a, ("zh",), lambda h: (1 - h,))
    both, behind, ahead, far, near = sync((both, behind, ahead, far, near))

    opposite = jnp.stack([along_y(behind[0], 1), along_y(ahead[1], -1)])
    far = spread(far, "x")
    near_c = permute(near, ("c",), lambda c: (1 - c,))
    opposite, far, near, near_c = sync((opposite, far, near, near_c))

    far_c = permute(far, ("c",), lambda c: (1 - c,))
    around = [both, ahead, opposite, behind]
    rows = ordered("y", [v[:, 0] for v in around]).reshape(64 * cols, tokens)
    input_grads = lax.dot_general(weight_codes, rows, (((1,), (0,)), ((), ())), preferred_element_type=jnp.float32)
    part = [[v[h, 1].reshape(2, 4 * cols, tokens) for v in around] for h in (0, 1)]
    weight_grads = 0.0
    for mine, blocks in (
        (jnp.stack([near, near_c], 1), part[0]),
        (far[:, None], [v[:1] for v in part[1]]),
        (far_c[:, None], [v[1:] for v in part[1]]),
    ):
        weight_grads += lax.dot_general(
            mine, ordered("y", blocks), (((0, 1, 3), (0, 1, 3)), ((), ())), preferred_element_type=jnp.float32
        )
    return input_grads.T, weight_grads


def solution(mesh):
    fine = Mesh(mesh.devices.reshape(SIZES), AXES)
    placed = (P(DP, TENSOR), P(TENSOR, None), P(), P(DP, TENSOR))
    return jax.shard_map(
        per_device,
        mesh=fine,
        in_specs=placed,
        out_specs=(P(DP, TENSOR), P(TENSOR, DP)),
        check_vma=False,
    )
```

```python
import itertools

import jax
import jax.numpy as jnp
import numpy as np
from jax import lax
from jax.sharding import Mesh, PartitionSpec as P

AXES = ("x", "zh", "c", "y", "za", "zb")
SIZES = (4, 2, 2, 4, 4, 4)
DP = ("x", "zh", "c")
TENSOR = ("y", "za", "zb")


def permute(value, axes, target):
    sizes = [SIZES[AXES.index(a)] for a in axes]
    pairs = []
    for place in itertools.product(*map(range, sizes)):
        to = target(*place)
        pairs.append((int(np.ravel_multi_index(place, sizes)), int(np.ravel_multi_index(to, sizes))))
    return lax.ppermute(value, axes, pairs)


def along_y(value, step):
    return permute(value, ("y",), lambda y: ((y + step) % 4,))


def spread(value, axis):
    n = SIZES[AXES.index(axis)]
    copies = jnp.broadcast_to(value[None], (n,) + value.shape)
    return lax.all_to_all(copies, axis, 0, 0, tiled=True)


def paired(value, bit):
    def flip(za, zb):
        z = (za * 4 + zb) ^ (8 >> bit)
        return (z // 4, z % 4)

    theirs = permute(value, ("za", "zb"), flip)
    place = lax.axis_index("za") * 4 + lax.axis_index("zb")
    low = (place >> (3 - bit)) % 2 == 0
    return jnp.where(low, jnp.stack([value, theirs], bit), jnp.stack([theirs, value], bit))


def ordered(axis, blocks):
    me = lax.axis_index(axis)
    ring = jnp.broadcast_to(blocks[0][None], (4,) + blocks[0].shape)
    for k, block in enumerate(blocks[1:], 1):
        ring = lax.dynamic_update_slice(ring, block[None], ((me + k) % 4,) + (0,) * block.ndim)
    return ring


sync = lax.optimization_barrier


def per_device(activations, weight_codes, channel_scale, output_grads):
    a = activations.T
    g = output_grads.T
    tokens = a.shape[1]
    cols = g.shape[0]
    half = 8 * cols

    me = lax.axis_index(TENSOR)
    scale = lax.dynamic_slice(channel_scale, (me * cols,), (cols,))
    scaled = (g.astype(jnp.float32) * scale[:, None]).astype(jnp.bfloat16)

    part = permute(g, AXES, lambda x, zh, c, y, za, zb: (y, za // 2, za % 2, x, 2 * zh + c, zb))
    far = permute(a, ("zh",), lambda h: (1 - h,))
    part, scaled, a, far = sync((part, scaled, a, far))

    both = jnp.concatenate([scaled, part])
    for bit in range(4):
        both, a, far = sync((paired(both, bit), a, far))
    both = both.reshape(16, 2, cols, tokens)
    rows = both[:, 0].reshape(2, half, tokens)
    part = both[:, 1].reshape(2, 2, 4 * cols, tokens)
    part = jnp.where(lax.axis_index("c") == 0, part, part[:, ::-1])
    part = jnp.where(lax.axis_index("zh") == 0, part, part[::-1])
    part = part.reshape(2, half, tokens)
    both = jnp.stack([rows, part], 1)
    both, a, far = sync((both, a, far))

    behind, ahead = along_y(both, 1), along_y(both, -1)
    acts = spread(jnp.stack([a, far]), "x")
    both, behind, ahead, acts = sync((both, behind, ahead, acts))

    opposite = jnp.stack([along_y(behind[0], 1), along_y(ahead[1], -1)])
    acts_c = permute(acts, ("c",), lambda c: (1 - c,))

    around = [both, ahead, opposite, behind]
    rows = ordered("y", [v[:, 0] for v in around]).reshape(64 * cols, tokens)
    input_grads = lax.dot_general(weight_codes, rows, (((1,), (0,)), ((), ())), preferred_element_type=jnp.float32)
    weight_grads = 0.0
    for half in (0, 1):
        mine = jnp.stack([acts[:, half], acts_c[:, half]], 1)
        blocks = ordered("y", [v[half, 1].reshape(2, 4 * cols, tokens) for v in around])
        weight_grads += lax.dot_general(
            mine, blocks, (((0, 1, 3), (0, 1, 3)), ((), ())), preferred_element_type=jnp.float32
        )
    return input_grads.T, weight_grads


def solution(mesh):
    fine = Mesh(mesh.devices.reshape(SIZES), AXES)
    placed = (P(DP, TENSOR), P(TENSOR, None), P(), P(DP, TENSOR))
    return jax.shard_map(
        per_device,
        mesh=fine,
        in_specs=placed,
        out_specs=(P(DP, TENSOR), P(TENSOR, DP)),
        check_vma=False,
    )
```

```python
import itertools

import jax
import jax.numpy as jnp
import numpy as np
from jax import lax
from jax.sharding import Mesh, PartitionSpec as P

AXES = ("x", "zh", "c", "y", "za", "zb")
SIZES = (4, 2, 2, 4, 4, 4)
DP = ("x", "zh", "c")
TENSOR = ("y", "za", "zb")


def permute(value, axes, target):
    sizes = [SIZES[AXES.index(a)] for a in axes]
    pairs = []
    for place in itertools.product(*map(range, sizes)):
        to = target(*place)
        pairs.append((int(np.ravel_multi_index(place, sizes)), int(np.ravel_multi_index(to, sizes))))
    return lax.ppermute(value, axes, pairs)


def along_y(value, step):
    return permute(value, ("y",), lambda y: ((y + step) % 4,))


def spread(value, axis):
    n = SIZES[AXES.index(axis)]
    copies = jnp.broadcast_to(value[None], (n,) + value.shape)
    return lax.all_to_all(copies, axis, 0, 0, tiled=True)


def paired(value, bit, axis):
    def flip(za, zb):
        z = (za * 4 + zb) ^ (8 >> bit)
        return (z // 4, z % 4)

    theirs = permute(value, ("za", "zb"), flip)
    place = lax.axis_index("za") * 4 + lax.axis_index("zb")
    low = (place >> (3 - bit)) % 2 == 0
    return jnp.where(low, jnp.stack([value, theirs], axis), jnp.stack([theirs, value], axis))


def ordered(axis, blocks):
    me = lax.axis_index(axis)
    ring = jnp.broadcast_to(blocks[0][None], (4,) + blocks[0].shape)
    for k, block in enumerate(blocks[1:], 1):
        ring = lax.dynamic_update_slice(ring, block[None], ((me + k) % 4,) + (0,) * block.ndim)
    return ring


sync = lax.optimization_barrier


def per_device(activations, weight_codes, channel_scale, output_grads):
    a = activations.T
    g = output_grads.T
    tokens = a.shape[1]
    cols = g.shape[0]
    half = 8 * cols

    me = lax.axis_index(TENSOR)
    scale = lax.dynamic_slice(channel_scale, (me * cols,), (cols,))
    scaled = (g.astype(jnp.float32) * scale[:, None]).astype(jnp.bfloat16)

    part = permute(g, AXES, lambda x, zh, c, y, za, zb: (y, za // 2, za % 2, x, 2 * zh + c, zb))
    far = permute(a, ("zh",), lambda h: (1 - h,))
    part, scaled = sync((part, scaled))

    both = jnp.concatenate([scaled, part])
    both, acts = sync((paired(both, 0, 0), jnp.stack([a, far])))
    both = both.reshape(2, 2, cols, tokens).transpose(1, 0, 2, 3)
    both = sync(paired(both, 1, 2))
    both = sync(paired(both, 2, 3))

    rows, part = sync((paired(both[0], 3, 3), both[1]))
    rows = rows.reshape(16 * cols, tokens)

    rows_b, rows_a = along_y(rows, 1), along_y(rows, -1)
    part = paired(part, 3, 3).reshape(2, 2, 4 * cols, tokens)
    part = jnp.where(lax.axis_index("c") == 0, part, part[:, ::-1])
    part = jnp.where(lax.axis_index("zh") == 0, part, part[::-1])
    part = part.reshape(16 * cols, tokens)
    rows_b, rows_a, part, acts = sync((rows_b, rows_a, part, acts))

    up = along_y(jnp.concatenate([rows_b[:half], part]), 1)
    down = along_y(jnp.concatenate([rows_a[half:], part]), -1)
    acts = spread(acts, "x")
    up, down, acts = sync((up, down, acts))
    rows_o = jnp.concatenate([up[:half], down[:half]])
    part_b, part_a = up[half:], down[half:]

    part_o = along_y(part_b[:half], 1), along_y(part_a[half:], -1)
    acts_c = permute(acts, ("c",), lambda c: (1 - c,))

    rows = ordered("y", [rows, rows_a, rows_o, rows_b]).reshape(64 * cols, tokens)
    input_grads = lax.dot_general(weight_codes, rows, (((1,), (0,)), ((), ())), preferred_element_type=jnp.float32)
    weight_grads = 0.0
    for i in (0, 1):
        mine = jnp.stack([acts[:, i], acts_c[:, i]], 1)
        own, ahead, behind = (v[i * half : (i + 1) * half] for v in (part, part_a, part_b))
        blocks = ordered("y", [v.reshape(2, 4 * cols, tokens) for v in (own, ahead, part_o[i], behind)])
        weight_grads += lax.dot_general(
            mine, blocks, (((0, 1, 3), (0, 1, 3)), ((), ())), preferred_element_type=jnp.float32
        )
    return input_grads.T, weight_grads


def solution(mesh):
    fine = Mesh(mesh.devices.reshape(SIZES), AXES)
    placed = (P(DP, TENSOR), P(TENSOR, None), P(), P(DP, TENSOR))
    return jax.shard_map(
        per_device,
        mesh=fine,
        in_specs=placed,
        out_specs=(P(DP, TENSOR), P(TENSOR, DP)),
        check_vma=False,
    )
```

```python
import itertools

import jax
import jax.numpy as jnp
import numpy as np
from jax import lax
from jax.sharding import Mesh, PartitionSpec as P

AXES = ("x", "zh", "c", "y", "za", "zb")
SIZES = (4, 2, 2, 4, 4, 4)
DP = ("x", "zh", "c")
TENSOR = ("y", "za", "zb")


def permute(value, axes, target):
    sizes = [SIZES[AXES.index(a)] for a in axes]
    pairs = []
    for place in itertools.product(*map(range, sizes)):
        to = target(*place)
        pairs.append((int(np.ravel_multi_index(place, sizes)), int(np.ravel_multi_index(to, sizes))))
    return lax.ppermute(value, axes, pairs)


def along_y(value, step):
    return permute(value, ("y",), lambda y: ((y + step) % 4,))


def spread(value, axis):
    n = SIZES[AXES.index(axis)]
    copies = jnp.broadcast_to(value[None], (n,) + value.shape)
    return lax.all_to_all(copies, axis, 0, 0, tiled=True)


def paired(value, bit, axis):
    def flip(za, zb):
        z = (za * 4 + zb) ^ (8 >> bit)
        return (z // 4, z % 4)

    theirs = permute(value, ("za", "zb"), flip)
    place = lax.axis_index("za") * 4 + lax.axis_index("zb")
    low = (place >> (3 - bit)) % 2 == 0
    return jnp.where(low, jnp.stack([value, theirs], axis), jnp.stack([theirs, value], axis))


def ordered(axis, blocks):
    me = lax.axis_index(axis)
    ring = jnp.broadcast_to(blocks[0][None], (4,) + blocks[0].shape)
    for k, block in enumerate(blocks[1:], 1):
        ring = lax.dynamic_update_slice(ring, block[None], ((me + k) % 4,) + (0,) * block.ndim)
    return ring


sync = lax.optimization_barrier


def per_device(activations, weight_codes, channel_scale, output_grads):
    a = activations.T
    g = output_grads.T
    tokens = a.shape[1]
    cols = g.shape[0]
    half = 8 * cols

    me = lax.axis_index(TENSOR)
    scale = lax.dynamic_slice(channel_scale, (me * cols,), (cols,))
    scaled = (g.astype(jnp.float32) * scale[:, None]).astype(jnp.bfloat16)

    part = permute(g, AXES, lambda x, zh, c, y, za, zb: (y, za // 2, za % 2, x, 2 * zh + c, zb))
    near = spread(a, "x")
    part, scaled, near, a = sync((part, scaled, near, a))

    both = jnp.concatenate([scaled, part])
    both = sync(paired(both, 0, 0))
    both = both.reshape(2, 2, cols, tokens).transpose(1, 0, 2, 3)
    both = sync(paired(both, 1, 2))
    both, a, near = sync((paired(both, 2, 3), a, near))

    rows, part, a = sync((paired(both[0], 3, 3), both[1], a))
    far = permute(a, ("zh",), lambda h: (1 - h,))
    rows = rows.reshape(16 * cols, tokens)

    rows_b, rows_a = along_y(rows, 1), along_y(rows, -1)
    part = paired(part, 3, 3).reshape(2, 2, 4 * cols, tokens)
    part = jnp.where(lax.axis_index("c") == 0, part, part[:, ::-1])
    part = jnp.where(lax.axis_index("zh") == 0, part, part[::-1])
    part = part.reshape(16 * cols, tokens)
    rows_b, rows_a, part = sync((rows_b, rows_a, part))

    up = along_y(jnp.concatenate([rows_b[:half], part]), 1)
    down = along_y(jnp.concatenate([rows_a[half:], part]), -1)
    near_c = permute(near, ("c",), lambda c: (1 - c,))
    up, down, far, near_c = sync((up, down, far, near_c))
    rows_o = jnp.concatenate([up[:half], down[:half]])
    part_b, part_a = up[half:], down[half:]

    part_o = along_y(part_b[:half], 1), along_y(part_a[half:], -1)
    far = spread(far, "x")
    far_c = permute(far, ("c",), lambda c: (1 - c,))
    rows = ordered("y", [rows, rows_a, rows_o, rows_b]).reshape(64 * cols, tokens)
    input_grads = lax.dot_general(weight_codes, rows, (((1,), (0,)), ((), ())), preferred_element_type=jnp.float32)
    weight_grads = 0.0
    for i in (0, 1):
        mine = jnp.stack([(near, far)[i], (near_c, far_c)[i]], 1)
        own, ahead, behind = (v[i * half : (i + 1) * half] for v in (part, part_a, part_b))
        blocks = ordered("y", [v.reshape(2, 4 * cols, tokens) for v in (own, ahead, part_o[i], behind)])
        weight_grads += lax.dot_general(
            mine, blocks, (((0, 1, 3), (0, 1, 3)), ((), ())), preferred_element_type=jnp.float32
        )
    return input_grads.T, weight_grads


def solution(mesh):
    fine = Mesh(mesh.devices.reshape(SIZES), AXES)
    placed = (P(DP, TENSOR), P(TENSOR, None), P(), P(DP, TENSOR))
    return jax.shard_map(
        per_device,
        mesh=fine,
        in_specs=placed,
        out_specs=(P(DP, TENSOR), P(TENSOR, DP)),
        check_vma=False,
    )
```

```python
import itertools

import jax
import jax.numpy as jnp
import numpy as np
from jax import lax
from jax.sharding import Mesh, PartitionSpec as P

AXES = ("x", "zh", "c", "y", "za", "zb")
SIZES = (4, 2, 2, 4, 4, 4)
DP = ("x", "zh", "c")
TENSOR = ("y", "za", "zb")


def permute(value, axes, target):
    sizes = [SIZES[AXES.index(a)] for a in axes]
    pairs = []
    for place in itertools.product(*map(range, sizes)):
        to = target(*place)
        pairs.append((int(np.ravel_multi_index(place, sizes)), int(np.ravel_multi_index(to, sizes))))
    return lax.ppermute(value, axes, pairs)


def along_y(value, step):
    return permute(value, ("y",), lambda y: ((y + step) % 4,))


def spread(value, axis):
    n = SIZES[AXES.index(axis)]
    copies = jnp.broadcast_to(value[None], (n,) + value.shape)
    return lax.all_to_all(copies, axis, 0, 0, tiled=True)


def paired(value, bit, axis):
    def flip(za, zb):
        z = (za * 4 + zb) ^ (8 >> bit)
        return (z // 4, z % 4)

    theirs = permute(value, ("za", "zb"), flip)
    place = lax.axis_index("za") * 4 + lax.axis_index("zb")
    low = (place >> (3 - bit)) % 2 == 0
    return jnp.where(low, jnp.stack([value, theirs], axis), jnp.stack([theirs, value], axis))


def ordered(axis, blocks):
    me = lax.axis_index(axis)
    ring = jnp.broadcast_to(blocks[0][None], (4,) + blocks[0].shape)
    for k, block in enumerate(blocks[1:], 1):
        ring = lax.dynamic_update_slice(ring, block[None], ((me + k) % 4,) + (0,) * block.ndim)
    return ring


sync = lax.optimization_barrier


def per_device(activations, weight_codes, channel_scale, output_grads):
    a = activations.T
    g = output_grads.T
    tokens = a.shape[1]
    cols = g.shape[0]
    half = 8 * cols

    me = lax.axis_index(TENSOR)
    scale = lax.dynamic_slice(channel_scale, (me * cols,), (cols,))
    scaled = (g.astype(jnp.float32) * scale[:, None]).astype(jnp.bfloat16)

    part = permute(g, AXES, lambda x, zh, c, y, za, zb: (y, za // 2, za % 2, x, 2 * zh + c, zb))
    part, scaled = sync((part, scaled))

    both = jnp.concatenate([scaled, part])
    both = sync(paired(both, 0, 0))
    both = both.reshape(2, 2, cols, tokens).transpose(1, 0, 2, 3)
    both = sync(paired(both, 1, 2))
    both, a = sync((paired(both, 2, 3), a))
    far = permute(a, ("zh",), lambda h: (1 - h,))

    rows, part = sync((paired(both[0], 3, 3), both[1]))
    rows = rows.reshape(16 * cols, tokens)

    rows_b, rows_a = along_y(rows, 1), along_y(rows, -1)
    part = paired(part, 3, 3).reshape(2, 2, 4 * cols, tokens)
    part = jnp.where(lax.axis_index("c") == 0, part, part[:, ::-1])
    part = jnp.where(lax.axis_index("zh") == 0, part, part[::-1])
    part = part.reshape(16 * cols, tokens)
    rows_b, rows_a, part, a, far = sync((rows_b, rows_a, part, a, far))

    up = along_y(jnp.concatenate([rows_b[:half], part]), 1)
    down = along_y(jnp.concatenate([rows_a[half:], part]), -1)
    acts = spread(jnp.stack([a, far]), "x")
    up, down, acts = sync((up, down, acts))
    rows_o = jnp.concatenate([up[:half], down[:half]])
    part_b, part_a = up[half:], down[half:]

    part_o = along_y(part_b[:half], 1), along_y(part_a[half:], -1)
    acts_c = permute(acts, ("c",), lambda c: (1 - c,))

    rows = ordered("y", [rows, rows_a, rows_o, rows_b]).reshape(64 * cols, tokens)
    input_grads = lax.dot_general(weight_codes, rows, (((1,), (0,)), ((), ())), preferred_element_type=jnp.float32)
    weight_grads = 0.0
    for i in (0, 1):
        mine = jnp.stack([acts[:, i], acts_c[:, i]], 1)
        own, ahead, behind = (v[i * half : (i + 1) * half] for v in (part, part_a, part_b))
        blocks = ordered("y", [v.reshape(2, 4 * cols, tokens) for v in (own, ahead, part_o[i], behind)])
        weight_grads += lax.dot_general(
            mine, blocks, (((0, 1, 3), (0, 1, 3)), ((), ())), preferred_element_type=jnp.float32
        )
    return input_grads.T, weight_grads


def solution(mesh):
    fine = Mesh(mesh.devices.reshape(SIZES), AXES)
    placed = (P(DP, TENSOR), P(TENSOR, None), P(), P(DP, TENSOR))
    return jax.shard_map(
        per_device,
        mesh=fine,
        in_specs=placed,
        out_specs=(P(DP, TENSOR), P(TENSOR, DP)),
        check_vma=False,
    )
```

```python
import itertools

import jax
import jax.numpy as jnp
import numpy as np
from jax import lax
from jax.sharding import Mesh, PartitionSpec as P

AXES = ("x", "zh", "c", "y", "za", "zb")
SIZES = (4, 2, 2, 4, 4, 4)
DP = ("x", "zh", "c")
TENSOR = ("y", "za", "zb")


def permute(value, axes, target):
    sizes = [SIZES[AXES.index(a)] for a in axes]
    pairs = []
    for place in itertools.product(*map(range, sizes)):
        to = target(*place)
        pairs.append((int(np.ravel_multi_index(place, sizes)), int(np.ravel_multi_index(to, sizes))))
    return lax.ppermute(value, axes, pairs)


def along_y(value, step):
    return permute(value, ("y",), lambda y: ((y + step) % 4,))


def spread(value, axis):
    n = SIZES[AXES.index(axis)]
    copies = jnp.broadcast_to(value[None], (n,) + value.shape)
    return lax.all_to_all(copies, axis, 0, 0, tiled=True)


def paired(value, bit, axis):
    def flip(za, zb):
        z = (za * 4 + zb) ^ (8 >> bit)
        return (z // 4, z % 4)

    theirs = permute(value, ("za", "zb"), flip)
    place = lax.axis_index("za") * 4 + lax.axis_index("zb")
    low = (place >> (3 - bit)) % 2 == 0
    return jnp.where(low, jnp.stack([value, theirs], axis), jnp.stack([theirs, value], axis))


def ordered(axis, blocks):
    me = lax.axis_index(axis)
    ring = jnp.broadcast_to(blocks[0][None], (4,) + blocks[0].shape)
    for k, block in enumerate(blocks[1:], 1):
        ring = lax.dynamic_update_slice(ring, block[None], ((me + k) % 4,) + (0,) * block.ndim)
    return ring


def product(left, right):
    return lax.dot_general(left, right, (((1,), (0,)), ((), ())), preferred_element_type=jnp.float32)


sync = lax.optimization_barrier


def per_device(activations, weight_codes, channel_scale, output_grads):
    a = activations.T
    g = output_grads.T
    tokens = a.shape[1]
    cols = g.shape[0]
    half = 8 * cols

    me = lax.axis_index(TENSOR)
    scale = lax.dynamic_slice(channel_scale, (me * cols,), (cols,))
    scaled = (g.astype(jnp.float32) * scale[:, None]).astype(jnp.bfloat16)

    part = permute(g, AXES, lambda x, zh, c, y, za, zb: (y, za // 2, za % 2, x, 2 * zh + c, zb))
    part, scaled = sync((part, scaled))

    both = jnp.concatenate([scaled, part])
    both = sync(paired(both, 0, 0))
    both = both.reshape(2, 2, cols, tokens).transpose(1, 0, 2, 3)
    both, near, a = sync((paired(both, 1, 2), spread(a, "x"), a))
    both, a = sync((paired(both, 2, 3), a))
    far = permute(a, ("zh",), lambda h: (1 - h,))

    rows, part = sync((paired(both[0], 3, 3), both[1]))
    rows = rows.reshape(16 * cols, tokens)

    rows_b, rows_a = along_y(rows, 1), along_y(rows, -1)
    part = paired(part, 3, 3).reshape(2, 2, 4 * cols, tokens)
    part = jnp.where(lax.axis_index("c") == 0, part, part[:, ::-1])
    part = jnp.where(lax.axis_index("zh") == 0, part, part[::-1])
    part = part.reshape(16 * cols, tokens)
    rows_b, rows_a, part, near, far = sync((rows_b, rows_a, part, near, far))

    up = along_y(jnp.concatenate([rows_b[:half], part]), 1)
    down = along_y(jnp.concatenate([rows_a[half:], part]), -1)
    far = spread(far, "x")
    near_c = permute(near, ("c",), lambda c: (1 - c,))
    three = ordered("y", [rows, rows_a, jnp.zeros_like(rows), rows_b]).reshape(64 * cols, tokens)
    input_grads = product(weight_codes, three)
    start = (lax.axis_index("y") + 2) % 4 * (16 * cols)
    fourth = lax.dynamic_slice(weight_codes, (0, start), (weight_codes.shape[0], 16 * cols))
    up, down, far, near_c, input_grads, fourth = sync((up, down, far, near_c, input_grads, fourth))
    rows_o = jnp.concatenate([up[:half], down[:half]])
    part_b, part_a = up[half:], down[half:]

    part_o = along_y(part_b[:half], 1), along_y(part_a[half:], -1)
    far_c = permute(far, ("c",), lambda c: (1 - c,))

    input_grads += product(fourth, rows_o)
    weight_grads = 0.0
    for i in (0, 1):
        mine = jnp.stack([(near, far)[i], (near_c, far_c)[i]], 1)
        own, ahead, behind = (v[i * half : (i + 1) * half] for v in (part, part_a, part_b))
        blocks = ordered("y", [v.reshape(2, 4 * cols, tokens) for v in (own, ahead, part_o[i], behind)])
        weight_grads += lax.dot_general(
            mine, blocks, (((0, 1, 3), (0, 1, 3)), ((), ())), preferred_element_type=jnp.float32
        )
    return input_grads.T, weight_grads


def solution(mesh):
    fine = Mesh(mesh.devices.reshape(SIZES), AXES)
    placed = (P(DP, TENSOR), P(TENSOR, None), P(), P(DP, TENSOR))
    return jax.shard_map(
        per_device,
        mesh=fine,
        in_specs=placed,
        out_specs=(P(DP, TENSOR), P(TENSOR, DP)),
        check_vma=False,
    )
```

```python
import itertools

import jax
import jax.numpy as jnp
import numpy as np
from jax import lax
from jax.sharding import Mesh, PartitionSpec as P

AXES = ("x", "zh", "c", "y", "za", "zb")
SIZES = (4, 2, 2, 4, 4, 4)
DP = ("x", "zh", "c")
TENSOR = ("y", "za", "zb")


def permute(value, axes, target):
    sizes = [SIZES[AXES.index(a)] for a in axes]
    pairs = []
    for place in itertools.product(*map(range, sizes)):
        to = target(*place)
        pairs.append((int(np.ravel_multi_index(place, sizes)), int(np.ravel_multi_index(to, sizes))))
    return lax.ppermute(value, axes, pairs)


def along_y(value, step):
    return permute(value, ("y",), lambda y: ((y + step) % 4,))


def spread(value, axis):
    n = SIZES[AXES.index(axis)]
    copies = jnp.broadcast_to(value[None], (n,) + value.shape)
    return lax.all_to_all(copies, axis, 0, 0, tiled=True)


def paired(value, bit, axis):
    def flip(za, zb):
        z = (za * 4 + zb) ^ (8 >> bit)
        return (z // 4, z % 4)

    theirs = permute(value, ("za", "zb"), flip)
    place = lax.axis_index("za") * 4 + lax.axis_index("zb")
    low = (place >> (3 - bit)) % 2 == 0
    return jnp.where(low, jnp.stack([value, theirs], axis), jnp.stack([theirs, value], axis))


def ordered(axis, blocks):
    me = lax.axis_index(axis)
    ring = jnp.broadcast_to(blocks[0][None], (4,) + blocks[0].shape)
    for k, block in enumerate(blocks[1:], 1):
        ring = lax.dynamic_update_slice(ring, block[None], ((me + k) % 4,) + (0,) * block.ndim)
    return ring


sync = lax.optimization_barrier


def per_device(activations, weight_codes, channel_scale, output_grads):
    a = activations.T
    g = output_grads.T
    tokens = a.shape[1]
    cols = g.shape[0]
    half = 8 * cols

    me = lax.axis_index(TENSOR)
    scale = lax.dynamic_slice(channel_scale, (me * cols,), (cols,))
    scaled = (g.astype(jnp.float32) * scale[:, None]).astype(jnp.bfloat16)

    part = permute(g, AXES, lambda x, zh, c, y, za, zb: (y, za // 2, za % 2, x, 2 * zh + c, zb))
    part, scaled = sync((part, scaled))

    both = jnp.concatenate([scaled, part])
    both = sync(paired(both, 0, 0))
    both = both.reshape(2, 2, cols, tokens).transpose(1, 0, 2, 3)
    both = sync(paired(both, 1, 2))
    both, a = sync((paired(both, 2, 3), a))
    far = permute(a, ("zh",), lambda h: (1 - h,))

    rows, part = sync((paired(both[0], 3, 3), both[1]))
    rows = rows.reshape(16 * cols, tokens)

    rows_b, rows_a = along_y(rows, 1), along_y(rows, -1)
    part = paired(part, 3, 3).reshape(2, 2, 4 * cols, tokens)
    part = jnp.where(lax.axis_index("c") == 0, part, part[:, ::-1])
    part = jnp.where(lax.axis_index("zh") == 0, part, part[::-1])
    part = part.reshape(16 * cols, tokens)
    rows_b, rows_a, part, a, far = sync((rows_b, rows_a, part, a, far))

    up = along_y(jnp.concatenate([rows_b[:half], part]), 1)
    down = along_y(jnp.concatenate([rows_a[half:], part]), -1)
    acts = spread(jnp.stack([a, far]), "x")
    up, down = sync((up, down))
    rows_o = jnp.concatenate([up[:half], down[:half]])
    part_b, part_a = up[half:], down[half:]

    part_o = along_y(part_b[:half], 1), along_y(part_a[half:], -1)
    acts_c = permute(acts, ("c",), lambda c: (1 - c,))

    rows = ordered("y", [rows, rows_a, rows_o, rows_b]).reshape(64 * cols, tokens)
    input_grads = lax.dot_general(weight_codes, rows, (((1,), (0,)), ((), ())), preferred_element_type=jnp.float32)
    weight_grads = 0.0
    for i in (0, 1):
        mine = jnp.stack([acts[:, i], acts_c[:, i]], 1)
        own, ahead, behind = (v[i * half : (i + 1) * half] for v in (part, part_a, part_b))
        blocks = ordered("y", [v.reshape(2, 4 * cols, tokens) for v in (own, ahead, part_o[i], behind)])
        weight_grads += lax.dot_general(
            mine, blocks, (((0, 1, 3), (0, 1, 3)), ((), ())), preferred_element_type=jnp.float32
        )
    return input_grads.T, weight_grads


def solution(mesh):
    fine = Mesh(mesh.devices.reshape(SIZES), AXES)
    placed = (P(DP, TENSOR), P(TENSOR, None), P(), P(DP, TENSOR))
    return jax.shard_map(
        per_device,
        mesh=fine,
        in_specs=placed,
        out_specs=(P(DP, TENSOR), P(TENSOR, DP)),
        check_vma=False,
    )
```

```python
import itertools

import jax
import jax.numpy as jnp
import numpy as np
from jax import lax
from jax.sharding import Mesh, PartitionSpec as P

AXES = ("x", "zh", "c", "y", "za", "zb")
SIZES = (4, 2, 2, 4, 4, 4)
DP = ("x", "zh", "c")
TENSOR = ("y", "za", "zb")


def permute(value, axes, target):
    sizes = [SIZES[AXES.index(a)] for a in axes]
    pairs = []
    for place in itertools.product(*map(range, sizes)):
        to = target(*place)
        pairs.append((int(np.ravel_multi_index(place, sizes)), int(np.ravel_multi_index(to, sizes))))
    return lax.ppermute(value, axes, pairs)


def along_y(value, step):
    return permute(value, ("y",), lambda y: ((y + step) % 4,))


def spread(value, axis):
    n = SIZES[AXES.index(axis)]
    copies = jnp.broadcast_to(value[None], (n,) + value.shape)
    return lax.all_to_all(copies, axis, 0, 0, tiled=True)


def paired(value, bit, axis):
    def flip(za, zb):
        z = (za * 4 + zb) ^ (8 >> bit)
        return (z // 4, z % 4)

    theirs = permute(value, ("za", "zb"), flip)
    place = lax.axis_index("za") * 4 + lax.axis_index("zb")
    low = (place >> (3 - bit)) % 2 == 0
    return jnp.where(low, jnp.stack([value, theirs], axis), jnp.stack([theirs, value], axis))


def ordered(axis, blocks):
    me = lax.axis_index(axis)
    ring = jnp.broadcast_to(blocks[0][None], (4,) + blocks[0].shape)
    for k, block in enumerate(blocks[1:], 1):
        ring = lax.dynamic_update_slice(ring, block[None], ((me + k) % 4,) + (0,) * block.ndim)
    return ring


sync = lax.optimization_barrier


def per_device(activations, weight_codes, channel_scale, output_grads):
    a = activations.T
    g = output_grads.T
    tokens = a.shape[1]
    cols = g.shape[0]
    half = 8 * cols

    me = lax.axis_index(TENSOR)
    scale = lax.dynamic_slice(channel_scale, (me * cols,), (cols,))
    scaled = (g.astype(jnp.float32) * scale[:, None]).astype(jnp.bfloat16)

    part = permute(g, AXES, lambda x, zh, c, y, za, zb: (y, za // 2, za % 2, x, 2 * zh + c, zb))
    part, scaled = sync((part, scaled))

    both = jnp.concatenate([scaled, part])
    both = sync(paired(both, 0, 0))
    both = both.reshape(2, 2, cols, tokens).transpose(1, 0, 2, 3)
    both = sync(paired(both, 1, 2))
    both, a = sync((paired(both, 2, 3), a))
    far = permute(a, ("zh",), lambda h: (1 - h,))

    rows, part = sync((paired(both[0], 3, 3), both[1]))
    rows = rows.reshape(16 * cols, tokens)

    rows_b, rows_a = along_y(rows, 1), along_y(rows, -1)
    part = paired(part, 3, 3).reshape(2, 2, 4 * cols, tokens)
    part = jnp.where(lax.axis_index("c") == 0, part, part[:, ::-1])
    part = jnp.where(lax.axis_index("zh") == 0, part, part[::-1])
    part = part.reshape(16 * cols, tokens)
    rows_b, rows_a, part, a = sync((rows_b, rows_a, part, a))
    far, kept = sync((far, part))

    up = along_y(jnp.concatenate([rows_b[:half], part]), 1)
    down = along_y(jnp.concatenate([rows_a[half:], part]), -1)
    acts = spread(jnp.stack([a, far]), "x")
    up, down = sync((up, down))
    rows_o = jnp.concatenate([up[:half], down[:half]])
    part_b, part_a = up[half:], down[half:]

    part_o = along_y(part_b[:half], 1), along_y(part_a[half:], -1)
    acts_c = permute(acts, ("c",), lambda c: (1 - c,))

    rows = ordered("y", [rows, rows_a, rows_o, rows_b]).reshape(64 * cols, tokens)
    input_grads = lax.dot_general(weight_codes, rows, (((1,), (0,)), ((), ())), preferred_element_type=jnp.float32)
    weight_grads = 0.0
    for i in (0, 1):
        mine = jnp.stack([acts[:, i], acts_c[:, i]], 1)
        own, ahead, behind = (v[i * half : (i + 1) * half] for v in (kept, part_a, part_b))
        blocks = ordered("y", [v.reshape(2, 4 * cols, tokens) for v in (own, ahead, part_o[i], behind)])
        weight_grads += lax.dot_general(
            mine, blocks, (((0, 1, 3), (0, 1, 3)), ((), ())), preferred_element_type=jnp.float32
        )
    return input_grads.T, weight_grads


def solution(mesh):
    fine = Mesh(mesh.devices.reshape(SIZES), AXES)
    placed = (P(DP, TENSOR), P(TENSOR, None), P(), P(DP, TENSOR))
    return jax.shard_map(
        per_device,
        mesh=fine,
        in_specs=placed,
        out_specs=(P(DP, TENSOR), P(TENSOR, DP)),
        check_vma=False,
    )
```

```python
import itertools

import jax
import jax.numpy as jnp
import numpy as np
from jax import lax
from jax.sharding import Mesh, PartitionSpec as P

AXES = ("x", "zh", "c", "y", "za", "zb")
SIZES = (4, 2, 2, 4, 4, 4)
DP = ("x", "zh", "c")
TENSOR = ("y", "za", "zb")


def permute(value, axes, target):
    sizes = [SIZES[AXES.index(a)] for a in axes]
    pairs = []
    for place in itertools.product(*map(range, sizes)):
        to = target(*place)
        pairs.append((int(np.ravel_multi_index(place, sizes)), int(np.ravel_multi_index(to, sizes))))
    return lax.ppermute(value, axes, pairs)


def along_y(value, step):
    return permute(value, ("y",), lambda y: ((y + step) % 4,))


def spread(value, axis):
    n = SIZES[AXES.index(axis)]
    copies = jnp.broadcast_to(value[None], (n,) + value.shape)
    return lax.all_to_all(copies, axis, 0, 0, tiled=True)


def paired(value, bit, axis):
    def flip(za, zb):
        z = (za * 4 + zb) ^ (8 >> bit)
        return (z // 4, z % 4)

    theirs = permute(value, ("za", "zb"), flip)
    place = lax.axis_index("za") * 4 + lax.axis_index("zb")
    low = (place >> (3 - bit)) % 2 == 0
    return jnp.where(low, jnp.stack([value, theirs], axis), jnp.stack([theirs, value], axis))


def ordered(axis, blocks):
    me = lax.axis_index(axis)
    ring = jnp.broadcast_to(blocks[0][None], (4,) + blocks[0].shape)
    for k, block in enumerate(blocks[1:], 1):
        ring = lax.dynamic_update_slice(ring, block[None], ((me + k) % 4,) + (0,) * block.ndim)
    return ring


sync = lax.optimization_barrier


def per_device(activations, weight_codes, channel_scale, output_grads):
    a = activations.T
    g = output_grads.T
    tokens = a.shape[1]
    cols = g.shape[0]
    half = 8 * cols

    me = lax.axis_index(TENSOR)
    scale = lax.dynamic_slice(channel_scale, (me * cols,), (cols,))
    scaled = (g.astype(jnp.float32) * scale[:, None]).astype(jnp.bfloat16)

    part = permute(g, AXES, lambda x, zh, c, y, za, zb: (y, za // 2, za % 2, x, 2 * zh + c, zb))
    part, scaled = sync((part, scaled))

    both = jnp.concatenate([scaled, part])
    both = sync(paired(both, 0, 0))
    both = both.reshape(2, 2, cols, tokens).transpose(1, 0, 2, 3)
    both = sync(paired(both, 1, 2))
    both, a = sync((paired(both, 2, 3), a))
    far = permute(a, ("zh",), lambda h: (1 - h,))

    rows, part = paired(both[0], 3, 3), both[1]
    rows = rows.reshape(16 * cols, tokens)

    rows_b, rows_a = along_y(rows, 1), along_y(rows, -1)
    part = paired(part, 3, 3).reshape(2, 2, 4 * cols, tokens)
    part = jnp.where(lax.axis_index("c") == 0, part, part[:, ::-1])
    part = jnp.where(lax.axis_index("zh") == 0, part, part[::-1])
    part = part.reshape(16 * cols, tokens)
    rows_b, rows_a, part, a = sync((rows_b, rows_a, part, a))
    far, kept = sync((far, part))

    up = along_y(jnp.concatenate([rows_b[:half], part]), 1)
    down = along_y(jnp.concatenate([rows_a[half:], part]), -1)
    acts = spread(jnp.stack([a, far]), "x")
    up, down = sync((up, down))
    rows_o = jnp.concatenate([up[:half], down[:half]])
    part_b, part_a = up[half:], down[half:]

    part_o = along_y(part_b[:half], 1), along_y(part_a[half:], -1)
    acts_c = permute(acts, ("c",), lambda c: (1 - c,))

    rows = ordered("y", [rows, rows_a, rows_o, rows_b]).reshape(64 * cols, tokens)
    input_grads = lax.dot_general(weight_codes, rows, (((1,), (0,)), ((), ())), preferred_element_type=jnp.float32)
    weight_grads = 0.0
    for i in (0, 1):
        mine = jnp.stack([acts[:, i], acts_c[:, i]], 1)
        own, ahead, behind = (v[i * half : (i + 1) * half] for v in (kept, part_a, part_b))
        blocks = ordered("y", [v.reshape(2, 4 * cols, tokens) for v in (own, ahead, part_o[i], behind)])
        weight_grads += lax.dot_general(
            mine, blocks, (((0, 1, 3), (0, 1, 3)), ((), ())), preferred_element_type=jnp.float32
        )
    return input_grads.T, weight_grads


def solution(mesh):
    fine = Mesh(mesh.devices.reshape(SIZES), AXES)
    placed = (P(DP, TENSOR), P(TENSOR, None), P(), P(DP, TENSOR))
    return jax.shard_map(
        per_device,
        mesh=fine,
        in_specs=placed,
        out_specs=(P(DP, TENSOR), P(TENSOR, DP)),
        check_vma=False,
    )
```
